32 devices in a mesh: seq: 8 (over y, x, core), chan: 4 (over z).
Axes of the slice: x: 2, y: 2, z: 4, core: 2. Of those that a mesh axis runs over, the one named last changes fastest.
Arguments:
- query_rows: bfloat16 [1024, 8192], P('seq', 'chan'), may hold values from -6 to 6
- key_rows: bfloat16 [1024, 8192], P('seq', 'chan'), may hold values from -6 to 6
- value_rows: bfloat16 [1024, 8192], P('seq', 'chan'), may hold values from -6 to 6
- grad_rows: bfloat16 [1024, 8192], P('seq', 'chan'), may hold values from -21 to 21
- filters: bfloat16 [512, 128], P('chan'), may hold values from -0.5 to 0.5
- span_order: int32 [16], replicated, may hold values from 0 to 15, as said below
Outputs:
- gated_out: bfloat16 [1024, 8192], P('seq', 'chan')
- grad_query: bfloat16 [1024, 8192], P('seq', 'chan')
- grad_key: bfloat16 [1024, 8192], P('seq', 'chan')
- grad_value: bfloat16 [1024, 8192], P('seq', 'chan')
- filter_grad: float32 [512, 128], P('chan')
The draws below stay inside these ranges and needn't reach their ends.
Inputs may be any that keep to these rules, and one draw needn't show every extreme that they name: span_order names every span once. Slot s lies on seq index s // 2, and span c is owned by seq index c // 2. Seq index i holds a span p below 8 in slot 2 * i and span 16 - 1 - p in slot 2 * i + 1; which p each index holds is drawn. No seq index holds two spans of one owner.
All inputs are finite; a program needn't handle non-finite values.
Results may differ from the reference program's by a relative error of at most 0.0085.
Values may be sent and summed in bfloat16 or wider, within the bound.
A program may use at most 128 MiB of HBM per device.

```python
import math
import jax
import jax.numpy as jnp
import numpy as np
from jax import lax

D = 8192
GROUP = 16
K = 128
GROUPS = 512
SPAN_ROWS = 64
TOKENS = 1024
SPANS = 16
N_SEQ = 8


def draw_grad_rows(key, part):
    first_key = jax.random.fold_in(key, 0)
    column = jnp.arange(D, dtype=jnp.float32) / D
    spread = jnp.power(10.0, column) / 3.0
    base = jnp.clip(jax.random.normal(first_key, (TOKENS, D), jnp.float32), -6.0, 6.0)
    values = base * spread[None, :]
    return values.astype(jnp.bfloat16)


def draw_span_order(key, part):
    order_key = jax.random.fold_in(key, 7)
    first = jax.random.permutation(order_key, jnp.arange(N_SEQ, dtype=jnp.int32)).astype(jnp.int32)
    second = (SPANS - 1 - first).astype(jnp.int32)
    return jnp.stack([first, second], axis=1).reshape(-1).astype(jnp.int32)


def block_levels(stream_key, shape, cuts, least, largest):
    factor_of, own = 1.0, jax.random.fold_in(stream_key, 6)
    for axis_at, parts in cuts:
        steps = jnp.exp(jax.random.uniform(jax.random.fold_in(own, axis_at), (parts,), jnp.float32, least / len(cuts), largest / len(cuts)))
        factor_of = factor_of * jnp.repeat(steps, shape[axis_at] // parts).reshape([-1 if axis == axis_at else 1 for axis in range(len(shape))])
    return factor_of


def normal_values(rng, shape, width, most, shards=(), kind=jnp.bfloat16):
    result = width * jax.random.normal(rng, shape, jnp.float32)
    if shards:
        result = result * block_levels(rng, shape, shards, -0.22, 0.18)
    return jnp.clip(result, -most, most).astype(kind)


def setup_inputs(seed: int = 0) -> dict:
    arg_keys = jax.random.split(jax.random.key(seed), 7)
    return {
        "query_rows": normal_values(arg_keys[0], (TOKENS, D), 1.0, 6.0, ((0, 8), (1, 4))),
        "key_rows": normal_values(arg_keys[1], (TOKENS, D), 1.0, 6.0, ((0, 8), (1, 4))),
        "value_rows": normal_values(arg_keys[2], (TOKENS, D), 1.0, 6.0, ((0, 8), (1, 4))),
        "grad_rows": draw_grad_rows(jax.random.fold_in(arg_keys[6], 71), 0),
        "filters": normal_values(arg_keys[4], (GROUPS, K), K ** -0.5, 0.5, ((0, 4),)),
        "span_order": draw_span_order(jax.random.fold_in(arg_keys[6], 71), 0),
    }


def band_tables(filters):
    taps = filters.shape[1]
    offsets = (np.arange(taps)[:, None] - np.arange(taps)[None, :]) % taps
    below = np.arange(taps)[:, None] >= np.arange(taps)[None, :]
    lookup = filters.astype(jnp.float32)[:, offsets]
    zeroed = jnp.zeros_like(lookup)
    return (jnp.where(below, lookup, zeroed), jnp.where(below, zeroed, lookup))

def times_rounded(left, right):
    return (left.astype(jnp.float32) * right.astype(jnp.float32)).astype(jnp.bfloat16)

def reference(query_rows, key_rows, value_rows, grad_rows, filters, span_order):

    def to_sequence(block):
        pieces = block.reshape(SPANS, SPAN_ROWS, D)
        return jnp.zeros_like(pieces).at[span_order].set(pieces).reshape(TOKENS, D)

    def to_slots(block):
        return block.reshape(SPANS, SPAN_ROWS, D)[span_order].reshape(TOKENS, D)
    highest = lax.Precision.HIGHEST
    queries = to_sequence(query_rows)
    keys_seq = to_sequence(key_rows)
    values_seq = to_sequence(value_rows)
    grads_seq = to_sequence(grad_rows)
    mixed_kv = times_rounded(keys_seq, values_seq)
    gated_grad = times_rounded(grads_seq, queries)
    main_band, wrap_band = band_tables(filters)
    zero_rows = jnp.zeros((K, D), jnp.float32)
    z_tiles = jnp.concatenate([zero_rows, mixed_kv.astype(jnp.float32)], axis=0).reshape(TOKENS // K + 1, K, GROUPS, GROUP)
    w_tiles = jnp.concatenate([gated_grad.astype(jnp.float32), zero_rows], axis=0).reshape(TOKENS // K + 1, K, GROUPS, GROUP)
    conv = jnp.einsum('gab,tbgc->tagc', main_band, z_tiles[1:], precision=highest)
    conv = conv + jnp.einsum('gab,tbgc->tagc', wrap_band, z_tiles[:-1], precision=highest)
    convolved = conv.reshape(TOKENS, D).astype(jnp.bfloat16)
    adjoint = jnp.einsum('gba,tbgc->tagc', main_band, w_tiles[:-1], precision=highest)
    adjoint = adjoint + jnp.einsum('gba,tbgc->tagc', wrap_band, w_tiles[1:], precision=highest)
    dmixed = adjoint.reshape(TOKENS, D).astype(jnp.bfloat16)
    main_corr = jnp.einsum('tagc,tbgc->gab', w_tiles[:-1], z_tiles[1:], precision=highest)
    wrap_corr = jnp.einsum('tagc,tbgc->gab', w_tiles[:-1], z_tiles[:-1], precision=highest)
    lag = np.arange(K)
    pick_main = (lag[:, None, None] - lag[None, :, None] == lag[None, None, :]).astype(np.float32)
    pick_wrap = (lag[:, None, None] - lag[None, :, None] + K == lag[None, None, :]).astype(np.float32)
    raw = jnp.einsum('gab,abj->gj', main_corr, jnp.asarray(pick_main, main_corr.dtype), precision=highest)
    raw = raw + jnp.einsum('gab,abj->gj', wrap_corr, jnp.asarray(pick_wrap, wrap_corr.dtype), precision=highest)
    squares = jnp.sum(raw * raw)
    limit = math.sqrt(GROUPS * K)
    factor = jnp.minimum(1.0, limit / jnp.sqrt(squares + 1e-06))
    filter_grad = factor * raw
    gated_out = to_slots(times_rounded(queries, convolved))
    grad_query = to_slots(times_rounded(grads_seq, convolved))
    grad_key = to_slots(times_rounded(dmixed, values_seq))
    grad_value = to_slots(times_rounded(dmixed, keys_seq))
    return (gated_out, grad_query, grad_key, grad_value, filter_grad)
```

```python
import functools
import math

import jax
import jax.numpy as jnp
from jax import lax
from jax.experimental import pallas as pl
from jax.experimental.pallas import tpu as pltpu
from jax.sharding import PartitionSpec as P

MESH = pl.DeviceIdType.MESH


def flip_bits(me, r, size):
    peer = me
    bit = 1
    while bit < size:
        if r & bit:
            peer = peer + bit - 2 * bit * (lax.div(me, bit) % 2)
        bit *= 2
    return peer


def kernel(
    n, m, taps, group, limit,
    order_ref, slot_ref, base_ref, q_ref, k_ref, v_ref, g_ref,
    go_ref, gq_ref, gk_ref, gv_ref, fg_ref,
    mix_send, gat_send, mix_recv, gat_recv, zseq, gseq, conv, dmix,
    conv_send, dmix_send, conv_ret, dmix_ret, bands, eacc, raws, norms,
    send_sem, recv_sem, norm_send, norm_recv,
):
    me = lax.axis_index("seq")
    line = lax.axis_index("chan")
    spans, span_rows, cw = mix_send.shape
    pd = spans // n
    rows = pd * span_rows
    _, halves, _, lanes = conv.shape
    tokens = spans * span_rows
    tiles = tokens // taps
    window = 2 * taps
    per_half = lanes // group
    groups = halves * per_half
    pair = 2 if lanes == 128 and tiles % 2 == 0 else 1
    steps = tiles // pair
    per_tile = taps // span_rows
    peers = sorted(range(1, n), key=lambda r: (r & 1, -bin(r).count("1")))

    barrier = pltpu.get_barrier_semaphore()
    for r in peers:
        pl.semaphore_signal(
            barrier, inc=1, device_id={"seq": flip_bits(me, r, n)}, device_id_type=MESH
        )
    for r in range(1, m):
        pl.semaphore_signal(
            barrier, inc=1, device_id={"chan": flip_bits(line, r, m)}, device_id_type=MESH
        )

    def exchange(kind, r, source, target):
        return pltpu.make_async_remote_copy(
            src_ref=source,
            dst_ref=target,
            send_sem=send_sem.at[kind, r],
            recv_sem=recv_sem.at[kind, r],
            device_id={"seq": flip_bits(me, r, n)},
            device_id_type=MESH,
        )

    def outward(kind, r, source, target):
        peer = flip_bits(me, r, n)
        return exchange(
            kind, r, source.at[pl.ds(peer * pd, pd)], target.at[pl.ds(me * pd, pd)]
        )

    def to_all(kind, r):
        return exchange(kind, r, raws.at[me], raws.at[me])

    def norm_copy(r):
        return pltpu.make_async_remote_copy(
            src_ref=norms.at[line],
            dst_ref=norms.at[line],
            send_sem=norm_send.at[r],
            recv_sem=norm_recv.at[r],
            device_id={"chan": flip_bits(line, r, m)},
            device_id_type=MESH,
        )

    def blocks(left, right, out):
        for d in range(n):
            cut = slice(d * cw, (d + 1) * cw)
            out[d * pd : (d + 1) * pd] = (left[:, cut] * right[:, cut]).reshape(pd, span_rows, cw)

    blocks(k_ref, v_ref, mix_send)
    pl.semaphore_wait(barrier, n + m - 2)
    for r in peers:
        outward(0, r, mix_send, mix_recv).start()
    blocks(g_ref, q_ref, gat_send)
    for r in peers:
        outward(1, r, gat_send, gat_recv).start()
    mix_recv[pl.ds(me * pd, pd)] = mix_send[pl.ds(me * pd, pd)]
    gat_recv[pl.ds(me * pd, pd)] = gat_send[pl.ds(me * pd, pd)]

    def build_band(i, carry):
        row = base_ref[pl.ds(i, 1), :]
        table = pltpu.roll(
            jnp.broadcast_to(row, (taps, window)), 0, 1, stride=1, stride_axis=0
        )
        bands[i] = table.astype(jnp.bfloat16)
        return carry

    lax.fori_loop(0, 2 * groups, build_band, 0)
    for h in range(halves):
        zseq[h, 0:taps] = jnp.zeros((taps, lanes), jnp.bfloat16)
        gseq[h, tokens : tokens + taps] = jnp.zeros((taps, lanes), jnp.bfloat16)

    column = lax.broadcasted_iota(jnp.int32, (taps, pair * lanes), 1)
    mine = [(column % lanes) // group == i for i in range(per_half)]

    def in_order(source, target, start):
        def step(c, carry):
            block = source[slot_ref[c]]
            at = pl.multiple_of(start + c * span_rows, span_rows)
            for h in range(halves):
                target[h, pl.ds(at, span_rows), :] = block[:, h * lanes : (h + 1) * lanes]
            return carry

        lax.fori_loop(0, spans, step, 0)

    def windows(source, h, u, length):
        parts = [
            source[h, pl.ds(pl.multiple_of((u * pair + p) * taps, taps), length), :]
            for p in range(pair)
        ]
        return parts[0] if pair == 1 else jnp.concatenate(parts, axis=1)

    def convolve(source, first_band, target):
        def step(i, carry):
            h, u = i // steps, i % steps
            weights = windows(source, h, u, window)
            total = jnp.zeros((taps, pair * lanes), jnp.float32)
            for g in range(per_half):
                part = jnp.dot(
                    bands[first_band + h * per_half + g], weights,
                    preferred_element_type=jnp.float32,
                )
                total = jnp.where(mine[g], part, total)
            total = total.astype(jnp.bfloat16)
            for p in range(pair):
                for b in range(per_tile):
                    target[(u * pair + p) * per_tile + b, h] = total[
                        b * span_rows : (b + 1) * span_rows, p * lanes : (p + 1) * lanes
                    ]
            return carry

        lax.fori_loop(0, halves * steps, step, 0)

    def in_slots(source, target):
        def step(s, carry):
            block = source[order_ref[s]]
            for h in range(halves):
                target[s, :, h * lanes : (h + 1) * lanes] = block[h]
            return carry

        lax.fori_loop(0, spans, step, 0)

    def send_back(kind, source, target):
        for r in peers:
            outward(kind, r, source, target).start()
        target[pl.ds(me * pd, pd)] = source[pl.ds(me * pd, pd)]

    for r in peers:
        outward(0, r, mix_send, mix_recv).wait_recv()
    in_order(mix_recv, zseq, taps)
    convolve(zseq, 0, conv)
    in_slots(conv, conv_send)
    send_back(2, conv_send, conv_ret)

    for r in peers:
        outward(1, r, gat_send, gat_recv).wait_recv()
    in_order(gat_recv, gseq, 0)
    convolve(gseq, groups, dmix)
    in_slots(dmix, dmix_send)
    send_back(3, dmix_send, dmix_ret)

    zero = jnp.zeros((taps, pair * lanes), jnp.bfloat16)
    row_at = lax.broadcasted_iota(jnp.int32, (per_half, 8, window), 1)
    for h in range(halves):
        eacc[...] = jnp.zeros_like(eacc)

        def correlate(u, carry):
            parts = [
                zseq[h, pl.ds(pl.multiple_of((u * pair + p + 1) * taps, taps), taps), :]
                for p in range(pair)
            ]
            here = parts[0] if pair == 1 else jnp.concatenate(parts, axis=1)
            ahead = windows(gseq, h, u, window)
            for g in range(per_half):
                eacc[g] += lax.dot_general(
                    jnp.where(mine[g], here, zero), ahead,
                    (((1,), (1,)), ((), ())), preferred_element_type=jnp.float32,
                )
            return carry

        lax.fori_loop(0, steps, correlate, 0)
        half = taps // 2
        left = eacc[...]
        while half >= 8:
            left = left[:, :half] + pltpu.roll(left[:, half:], window - half, 2)
            half //= 2
        while half >= 1:
            left = jnp.where((row_at // half) % 2 == 1, pltpu.roll(left, window - half, 2), left)
            half //= 2
        raws[me, h * per_half : (h + 1) * per_half] = jnp.sum(left, axis=1)[:, :taps]

    for r in peers:
        to_all(4, r).start()

    for r in peers:
        to_all(4, r).wait_recv()
    norms[line] = jnp.full(norms.shape[1:], jnp.sum(raws[...] * raws[...]), jnp.float32)
    for r in range(1, m):
        norm_copy(r).start()

    def products(returned, first, first_out, second, second_out):
        for d in range(n):
            cut = slice(d * cw, (d + 1) * cw)
            block = returned[d * pd : (d + 1) * pd].reshape(rows, cw)
            first_out[:, cut] = first[:, cut] * block
            second_out[:, cut] = second[:, cut] * block

    for r in peers:
        outward(2, r, conv_send, conv_ret).wait_recv()
    products(conv_ret, q_ref, go_ref, g_ref, gq_ref)
    for r in peers:
        outward(3, r, dmix_send, dmix_ret).wait_recv()
    products(dmix_ret, v_ref, gk_ref, k_ref, gv_ref)

    for r in range(1, m):
        norm_copy(r).wait_recv()
    squares = norms[0]
    for i in range(1, m):
        squares = squares + norms[i]
    factor = jnp.minimum(1.0, limit / jnp.sqrt(squares[0:1, :] + 1e-06))
    for d in range(n):
        fg_ref[d * groups : (d + 1) * groups, :] = raws[d] * factor[:, :taps]

    for kind, (source, target) in enumerate(
        ((mix_send, mix_recv), (gat_send, gat_recv), (conv_send, conv_ret), (dmix_send, dmix_ret))
    ):
        for r in peers:
            outward(kind, r, source, target).wait_send()
    for r in peers:
        to_all(4, r).wait_send()
    for r in range(1, m):
        norm_copy(r).wait_send()


def shards(n, m, query_rows, key_rows, value_rows, grad_rows, filters, span_order):
    rows, channels = query_rows.shape
    all_groups, taps = filters.shape
    group = channels // all_groups
    spans = span_order.shape[0]
    span_rows = rows * n // spans
    cw = channels // n
    lanes = min(128, cw)
    halves = cw // lanes
    groups = all_groups // n
    tokens = rows * n
    own = lax.dynamic_slice_in_dim(filters, lax.axis_index("seq") * groups, groups, 0)
    own = own.astype(jnp.float32)
    base = jnp.concatenate(
        [
            jnp.pad(own[:, ::-1], ((0, 0), (1, taps - 1))),
            jnp.pad(own, ((0, 0), (0, taps))),
        ],
        axis=0,
    )
    place = jnp.arange(spans, dtype=jnp.int32)
    held = span_order[None, :] == place[:, None]
    slots = jnp.sum(jnp.where(held, place[None, :], 0), axis=1, dtype=jnp.int32)
    block = pltpu.VMEM((spans, span_rows, cw), jnp.bfloat16)
    ordered = pltpu.VMEM((halves, tokens + taps, lanes), jnp.bfloat16)
    result = pltpu.VMEM((spans, halves, span_rows, lanes), jnp.bfloat16)
    vmem = pl.BlockSpec(memory_space=pltpu.VMEM)
    limit = math.sqrt(all_groups * m * taps)
    like = jax.ShapeDtypeStruct((rows, channels), jnp.bfloat16)
    return pl.pallas_call(
        functools.partial(kernel, n, m, taps, group, limit),
        out_shape=(like, like, like, like, jax.ShapeDtypeStruct((all_groups, taps), jnp.float32)),
        in_specs=[pl.BlockSpec(memory_space=pltpu.SMEM)] * 2 + [vmem] * 5,
        out_specs=(vmem,) * 5,
        scratch_shapes=[
            block, block, block, block, ordered, ordered, result, result,
            block, block, block, block,
            pltpu.VMEM((2 * groups, taps, 2 * taps), jnp.bfloat16),
            pltpu.VMEM((lanes // group, taps, 2 * taps), jnp.float32),
            pltpu.VMEM((n, groups, taps), jnp.float32),
            pltpu.VMEM((m, 8, 128), jnp.float32),
            pltpu.SemaphoreType.DMA((5, n)),
            pltpu.SemaphoreType.DMA((5, n)),
            pltpu.SemaphoreType.DMA((m,)),
            pltpu.SemaphoreType.DMA((m,)),
        ],
        compiler_params=pltpu.CompilerParams(
            collective_id=0, has_side_effects=True, vmem_limit_bytes=48 * 1024 * 1024
        ),
    )(span_order, slots, base, query_rows, key_rows, value_rows, grad_rows)


def solution(mesh):
    rows = P("seq", "chan")
    return jax.shard_map(
        functools.partial(shards, mesh.shape["seq"], mesh.shape["chan"]),
        mesh=mesh,
        in_specs=(rows, rows, rows, rows, P("chan", None), P()),
        out_specs=(rows, rows, rows, rows, P("chan", None)),
        check_vma=False,
    )
```

```python
import functools
import math

import jax
import jax.numpy as jnp
from jax import lax
from jax.experimental import pallas as pl
from jax.experimental.pallas import tpu as pltpu
from jax.sharding import PartitionSpec as P

MESH = pl.DeviceIdType.MESH


def flip_bits(me, r, size):
    peer = me
    bit = 1
    while bit < size:
        if r & bit:
            peer = peer + bit - 2 * bit * (lax.div(me, bit) % 2)
        bit *= 2
    return peer


def kernel(
    n, m, taps, group, limit,
    order_ref, slot_ref, base_ref, q_in, k_in, v_in, g_in,
    go_ref, gq_ref, gk_ref, gv_ref, fg_ref,
    mix_send, gat_send, mix_recv, gat_recv, zseq, gseq, conv, dmix,
    conv_send, dmix_send, conv_ret, dmix_ret, bands, eacc, raws, norms,
    send_sem, recv_sem, norm_send, norm_recv, q_ref, k_ref, v_ref, g_ref, load_sem,
):
    me = lax.axis_index("seq")
    line = lax.axis_index("chan")
    spans, span_rows, cw = mix_send.shape
    pd = spans // n
    rows = pd * span_rows
    _, halves, _, lanes = conv.shape
    tokens = spans * span_rows
    tiles = tokens // taps
    window = 2 * taps
    per_half = lanes // group
    groups = halves * per_half
    pair = 2 if lanes == 128 and tiles % 2 == 0 else 1
    steps = tiles // pair
    per_tile = taps // span_rows
    peers = sorted(range(1, n), key=lambda r: (r & 1, -bin(r).count("1")))

    loads = [
        pltpu.make_async_copy(source, target, load_sem.at[i])
        for i, (source, target) in enumerate(
            ((k_in, k_ref), (v_in, v_ref), (g_in, g_ref), (q_in, q_ref))
        )
    ]
    for load in loads:
        load.start()
    barrier = pltpu.get_barrier_semaphore()
    for r in peers:
        pl.semaphore_signal(
            barrier, inc=1, device_id={"seq": flip_bits(me, r, n)}, device_id_type=MESH
        )
    for r in range(1, m):
        pl.semaphore_signal(
            barrier, inc=1, device_id={"chan": flip_bits(line, r, m)}, device_id_type=MESH
        )

    def exchange(kind, r, source, target):
        return pltpu.make_async_remote_copy(
            src_ref=source,
            dst_ref=target,
            send_sem=send_sem.at[kind, r],
            recv_sem=recv_sem.at[kind, r],
            device_id={"seq": flip_bits(me, r, n)},
            device_id_type=MESH,
        )

    def outward(kind, r, source, target):
        peer = flip_bits(me, r, n)
        return exchange(
            kind, r, source.at[pl.ds(peer * pd, pd)], target.at[pl.ds(me * pd, pd)]
        )

    def to_all(kind, r):
        return exchange(kind, r, raws.at[me], raws.at[me])

    def norm_copy(r):
        return pltpu.make_async_remote_copy(
            src_ref=norms.at[line],
            dst_ref=norms.at[line],
            send_sem=norm_send.at[r],
            recv_sem=norm_recv.at[r],
            device_id={"chan": flip_bits(line, r, m)},
            device_id_type=MESH,
        )

    def blocks(left, right, out):
        for d in range(n):
            cut = slice(d * cw, (d + 1) * cw)
            out[d * pd : (d + 1) * pd] = (left[:, cut] * right[:, cut]).reshape(pd, span_rows, cw)

    loads[0].wait()
    loads[1].wait()
    blocks(k_ref, v_ref, mix_send)
    pl.semaphore_wait(barrier, n + m - 2)
    for r in peers:
        outward(0, r, mix_send, mix_recv).start()
    loads[2].wait()
    loads[3].wait()
    blocks(g_ref, q_ref, gat_send)
    for r in peers:
        outward(1, r, gat_send, gat_recv).start()
    mix_recv[pl.ds(me * pd, pd)] = mix_send[pl.ds(me * pd, pd)]
    gat_recv[pl.ds(me * pd, pd)] = gat_send[pl.ds(me * pd, pd)]

    def build_band(i, carry):
        row = base_ref[pl.ds(i, 1), :]
        table = pltpu.roll(
            jnp.broadcast_to(row, (taps, window)), 0, 1, stride=1, stride_axis=0
        )
        bands[i] = table.astype(jnp.bfloat16)
        return carry

    lax.fori_loop(0, 2 * groups, build_band, 0)
    for h in range(halves):
        zseq[h, 0:taps] = jnp.zeros((taps, lanes), jnp.bfloat16)
        gseq[h, tokens : tokens + taps] = jnp.zeros((taps, lanes), jnp.bfloat16)

    column = lax.broadcasted_iota(jnp.int32, (taps, pair * lanes), 1)
    mine = [(column % lanes) // group == i for i in range(per_half)]

    def in_order(source, target, start):
        def step(c, carry):
            block = source[slot_ref[c]]
            at = pl.multiple_of(start + c * span_rows, span_rows)
            for h in range(halves):
                target[h, pl.ds(at, span_rows), :] = block[:, h * lanes : (h + 1) * lanes]
            return carry

        lax.fori_loop(0, spans, step, 0)

    def windows(source, h, u, length):
        parts = [
            source[h, pl.ds(pl.multiple_of((u * pair + p) * taps, taps), length), :]
            for p in range(pair)
        ]
        return parts[0] if pair == 1 else jnp.concatenate(parts, axis=1)

    def convolve(source, first_band, target):
        def step(i, carry):
            h, u = i // steps, i % steps
            weights = windows(source, h, u, window)
            total = jnp.zeros((taps, pair * lanes), jnp.float32)
            for g in range(per_half):
                part = jnp.dot(
                    bands[first_band + h * per_half + g], weights,
                    preferred_element_type=jnp.float32,
                )
                total = jnp.where(mine[g], part, total)
            total = total.astype(jnp.bfloat16)
            for p in range(pair):
                for b in range(per_tile):
                    target[(u * pair + p) * per_tile + b, h] = total[
                        b * span_rows : (b + 1) * span_rows, p * lanes : (p + 1) * lanes
                    ]
            return carry

        lax.fori_loop(0, halves * steps, step, 0)

    def in_slots(source, target):
        def step(s, carry):
            block = source[order_ref[s]]
            for h in range(halves):
                target[s, :, h * lanes : (h + 1) * lanes] = block[h]
            return carry

        lax.fori_loop(0, spans, step, 0)

    def send_back(kind, source, target):
        for r in peers:
            outward(kind, r, source, target).start()
        target[pl.ds(me * pd, pd)] = source[pl.ds(me * pd, pd)]

    for r in peers:
        outward(0, r, mix_send, mix_recv).wait_recv()
    in_order(mix_recv, zseq, taps)
    convolve(zseq, 0, conv)
    in_slots(conv, conv_send)
    send_back(2, conv_send, conv_ret)

    for r in peers:
        outward(1, r, gat_send, gat_recv).wait_recv()
    in_order(gat_recv, gseq, 0)
    convolve(gseq, groups, dmix)
    in_slots(dmix, dmix_send)
    send_back(3, dmix_send, dmix_ret)

    zero = jnp.zeros((taps, pair * lanes), jnp.bfloat16)
    row_at = lax.broadcasted_iota(jnp.int32, (per_half, 8, window), 1)
    for h in range(halves):
        eacc[...] = jnp.zeros_like(eacc)

        def correlate(u, carry):
            parts = [
                zseq[h, pl.ds(pl.multiple_of((u * pair + p + 1) * taps, taps), taps), :]
                for p in range(pair)
            ]
            here = parts[0] if pair == 1 else jnp.concatenate(parts, axis=1)
            ahead = windows(gseq, h, u, window)
            for g in range(per_half):
                eacc[g] += lax.dot_general(
                    jnp.where(mine[g], here, zero), ahead,
                    (((1,), (1,)), ((), ())), preferred_element_type=jnp.float32,
                )
            return carry

        lax.fori_loop(0, steps, correlate, 0)
        half = taps // 2
        left = eacc[...]
        while half >= 8:
            left = left[:, :half] + pltpu.roll(left[:, half:], window - half, 2)
            half //= 2
        while half >= 1:
            left = jnp.where((row_at // half) % 2 == 1, pltpu.roll(left, window - half, 2), left)
            half //= 2
        raws[me, h * per_half : (h + 1) * per_half] = jnp.sum(left, axis=1)[:, :taps]

    for r in peers:
        to_all(4, r).start()

    for r in peers:
        to_all(4, r).wait_recv()
    norms[line] = jnp.full(norms.shape[1:], jnp.sum(raws[...] * raws[...]), jnp.float32)
    for r in range(1, m):
        norm_copy(r).start()

    def products(returned, first, first_out, second, second_out):
        for d in range(n):
            cut = slice(d * cw, (d + 1) * cw)
            block = returned[d * pd : (d + 1) * pd].reshape(rows, cw)
            first_out[:, cut] = first[:, cut] * block
            second_out[:, cut] = second[:, cut] * block

    for r in peers:
        outward(2, r, conv_send, conv_ret).wait_recv()
    products(conv_ret, q_ref, go_ref, g_ref, gq_ref)
    for r in peers:
        outward(3, r, dmix_send, dmix_ret).wait_recv()
    products(dmix_ret, v_ref, gk_ref, k_ref, gv_ref)

    for r in range(1, m):
        norm_copy(r).wait_recv()
    squares = norms[0]
    for i in range(1, m):
        squares = squares + norms[i]
    factor = jnp.minimum(1.0, limit / jnp.sqrt(squares[0:1, :] + 1e-06))
    for d in range(n):
        fg_ref[d * groups : (d + 1) * groups, :] = raws[d] * factor[:, :taps]

    for kind, (source, target) in enumerate(
        ((mix_send, mix_recv), (gat_send, gat_recv), (conv_send, conv_ret), (dmix_send, dmix_ret))
    ):
        for r in peers:
            outward(kind, r, source, target).wait_send()
    for r in peers:
        to_all(4, r).wait_send()
    for r in range(1, m):
        norm_copy(r).wait_send()


def shards(n, m, query_rows, key_rows, value_rows, grad_rows, filters, span_order):
    rows, channels = query_rows.shape
    all_groups, taps = filters.shape
    group = channels // all_groups
    spans = span_order.shape[0]
    span_rows = rows * n // spans
    cw = channels // n
    lanes = min(128, cw)
    halves = cw // lanes
    groups = all_groups // n
    tokens = rows * n
    own = lax.dynamic_slice_in_dim(filters, lax.axis_index("seq") * groups, groups, 0)
    own = own.astype(jnp.float32)
    base = jnp.concatenate(
        [
            jnp.pad(own[:, ::-1], ((0, 0), (1, taps - 1))),
            jnp.pad(own, ((0, 0), (0, taps))),
        ],
        axis=0,
    )
    place = jnp.arange(spans, dtype=jnp.int32)
    held = span_order[None, :] == place[:, None]
    slots = jnp.sum(jnp.where(held, place[None, :], 0), axis=1, dtype=jnp.int32)
    block = pltpu.VMEM((spans, span_rows, cw), jnp.bfloat16)
    ordered = pltpu.VMEM((halves, tokens + taps, lanes), jnp.bfloat16)
    result = pltpu.VMEM((spans, halves, span_rows, lanes), jnp.bfloat16)
    vmem = pl.BlockSpec(memory_space=pltpu.VMEM)
    limit = math.sqrt(all_groups * m * taps)
    like = jax.ShapeDtypeStruct((rows, channels), jnp.bfloat16)
    return pl.pallas_call(
        functools.partial(kernel, n, m, taps, group, limit),
        out_shape=(like, like, like, like, jax.ShapeDtypeStruct((all_groups, taps), jnp.float32)),
        in_specs=[pl.BlockSpec(memory_space=pltpu.SMEM)] * 2
        + [vmem]
        + [pl.BlockSpec(memory_space=pl.ANY)] * 4,
        out_specs=(vmem,) * 5,
        scratch_shapes=[
            block, block, block, block, ordered, ordered, result, result,
            block, block, block, block,
            pltpu.VMEM((2 * groups, taps, 2 * taps), jnp.bfloat16),
            pltpu.VMEM((lanes // group, taps, 2 * taps), jnp.float32),
            pltpu.VMEM((n, groups, taps), jnp.float32),
            pltpu.VMEM((m, 8, 128), jnp.float32),
            pltpu.SemaphoreType.DMA((5, n)),
            pltpu.SemaphoreType.DMA((5, n)),
            pltpu.SemaphoreType.DMA((m,)),
            pltpu.SemaphoreType.DMA((m,)),
            pltpu.VMEM((rows, channels), jnp.bfloat16),
            pltpu.VMEM((rows, channels), jnp.bfloat16),
            pltpu.VMEM((rows, channels), jnp.bfloat16),
            pltpu.VMEM((rows, channels), jnp.bfloat16),
            pltpu.SemaphoreType.DMA((4,)),
        ],
        compiler_params=pltpu.CompilerParams(
            collective_id=0, has_side_effects=True, vmem_limit_bytes=48 * 1024 * 1024
        ),
    )(span_order, slots, base, query_rows, key_rows, value_rows, grad_rows)


def solution(mesh):
    rows = P("seq", "chan")
    return jax.shard_map(
        functools.partial(shards, mesh.shape["seq"], mesh.shape["chan"]),
        mesh=mesh,
        in_specs=(rows, rows, rows, rows, P("chan", None), P()),
        out_specs=(rows, rows, rows, rows, P("chan", None)),
        check_vma=False,
    )
```
